128 devices in a mesh: row: 4 (over z), col: 16 (over x, y), depth: 2 (over core).
Axes of the slice: x: 4, y: 4, z: 4, core: 2. Of those that a mesh axis runs over, the one named last changes fastest.
Arguments:
- tiles: float32 [4, 16, 96, 256, 256], P('row', 'col', 'depth'), as said below
- tile_rows: int32 [4, 16, 96], P('row', 'col', 'depth'), may hold values from 0 to 127, as said below
- tile_cols: int32 [4, 16, 96], P('row', 'col', 'depth'), may hold values from 0 to 127
- tile_count: int32 [4, 16, 2], P('row', 'col', 'depth'), may hold values from 16 to 48, as said below
Outputs:
- row_scale: float32 [131072], P('row')
- col_scale: float32 [524288], P('col')
- scaled_tiles: float32 [4, 16, 96, 256, 256], P('row', 'col', 'depth')
The draws below stay inside these ranges and needn't reach their ends.
Inputs may be any that keep to these rules, and one draw needn't show every extreme that they name: `tile_rows`: every block row and every block column of the matrix holds a live tile; no block is listed twice among the live tiles of the two depth lists of one row and col index. `tile_count`: some device's list is full in every draw. `tiles`: entries in empty slots are ignored.
All inputs are finite; a program needn't handle non-finite values.
Results may differ from the reference program's by a relative error of at most 0.0001.
Values sent between devices are 32-bit elements; how exact they have to be, the bound alone decides.
No kernel may reach another device: no remote copies, remote signals or barrier semaphores. Data moves between devices by JAX's collectives and lax.ppermute only.
A program may use at most 128 MiB of HBM per device.

```python
import math
import jax
import jax.numpy as jnp
from jax import lax

TILE = 256
RB_DEV = 128
ANCHORS = 16
SWEEPS = 4
SLOTS = 48
CB_DEV = 128
ROW_GROUPS = 4
COL_GROUPS = 16
DEPTH_SPLIT = 2


def pattern(key):
    base_key = jax.random.fold_in(key, 7)
    key_extra, key_order, key_count = jax.random.split(base_key, 3)
    groups_row = ROW_GROUPS
    groups_col = COL_GROUPS
    depths = DEPTH_SPLIT
    row_pos = jnp.arange(groups_row, dtype=jnp.int32)[:, None, None, None]
    col_pos = jnp.arange(groups_col, dtype=jnp.int32)[None, :, None, None]
    depth_pos = jnp.arange(depths, dtype=jnp.int32)[None, None, :, None]
    anchor_ids = jnp.arange(ANCHORS, dtype=jnp.int32)[None, None, None, :]
    shape_four = (groups_row, groups_col, depths, ANCHORS)
    anchor_cols = jnp.broadcast_to((row_pos * depths + depth_pos) * ANCHORS + anchor_ids, shape_four)
    extra_cols = jax.random.randint(key_extra, (groups_row, groups_col, depths, 2 * ANCHORS), 0, CB_DEV).astype(jnp.int32)
    all_cols = jnp.concatenate([anchor_cols, extra_cols], axis=3)
    window_start = col_pos * depths * ANCHORS
    anchor_spot = jnp.broadcast_to(window_start + depth_pos * ANCHORS + anchor_ids, shape_four)
    second_spot = jnp.broadcast_to(window_start + depths * ANCHORS + depth_pos * ANCHORS + anchor_ids, shape_four)
    third_spot = jnp.broadcast_to(window_start + depths * ANCHORS + (depths + depth_pos) * ANCHORS + anchor_ids, shape_four)
    spots = jnp.concatenate([anchor_spot, second_spot, third_spot], axis=3) % RB_DEV
    order_keys = jax.random.split(key_order, groups_row)
    row_order = jax.vmap(lambda one_key: jax.random.permutation(one_key, RB_DEV))(order_keys).astype(jnp.int32)
    flat_spots = spots.reshape(groups_row, groups_col * depths * SLOTS)
    all_rows = jnp.take_along_axis(row_order, flat_spots, axis=1)
    all_rows = all_rows.reshape(groups_row, groups_col, depths * SLOTS).astype(jnp.int32)
    all_cols = all_cols.reshape(groups_row, groups_col, depths * SLOTS).astype(jnp.int32)
    level = jax.random.randint(key_count, (groups_row, groups_col, depths), 0, 2 * ANCHORS + 1).astype(jnp.int32)
    extra = level * level * level // (4 * ANCHORS * ANCHORS)
    counts = ANCHORS + extra
    chosen = jax.random.randint(jax.random.fold_in(key_count, 1), (), 0, groups_row * groups_col * depths).astype(jnp.int32)
    flat_ids = jnp.arange(groups_row * groups_col * depths, dtype=jnp.int32).reshape(groups_row, groups_col, depths)
    counts = jnp.where(flat_ids == chosen, jnp.int32(SLOTS), counts).astype(jnp.int32)
    return (all_rows, all_cols, counts)


def draw_tile_rows(key, part):
    return pattern(key)[0]


def draw_tile_cols(key, part):
    return pattern(key)[1]


def draw_tile_count(key, part):
    return pattern(key)[2]


def draw_tiles(key, part):
    key_values, key_rowscale, key_colscale = jax.random.split(jax.random.fold_in(key, 11), 3)
    shape_all = (ROW_GROUPS, COL_GROUPS, DEPTH_SPLIT * SLOTS, TILE, TILE)
    shape_rowscale = (ROW_GROUPS, COL_GROUPS, DEPTH_SPLIT * SLOTS, TILE, 1)
    shape_colscale = (ROW_GROUPS, COL_GROUPS, DEPTH_SPLIT * SLOTS, 1, TILE)
    entries = jax.random.normal(key_values, shape_all, jnp.float32)
    reach = math.log(30.0)
    row_spread = jnp.exp(jax.random.uniform(key_rowscale, shape_rowscale, jnp.float32, 0.0, reach))
    col_spread = jnp.exp(jax.random.uniform(key_colscale, shape_colscale, jnp.float32, 0.0, reach))
    return (entries * row_spread * col_spread).astype(jnp.float32)


def setup_inputs(seed: int = 0) -> dict:
    arg_keys = jax.random.split(jax.random.key(seed), 5)
    tiles = draw_tiles(jax.random.fold_in(arg_keys[4], 71), 0)
    tile_rows = draw_tile_rows(jax.random.fold_in(arg_keys[4], 71), 0)
    tile_cols = draw_tile_cols(jax.random.fold_in(arg_keys[4], 71), 0)
    tile_count = draw_tile_count(jax.random.fold_in(arg_keys[4], 71), 0)
    return dict(tiles=tiles, tile_rows=tile_rows, tile_cols=tile_cols, tile_count=tile_count)


EPS = 1e-06

def reference(tiles, tile_rows, tile_cols, tile_count):
    groups_row = ROW_GROUPS
    groups_col = COL_GROUPS
    slot_total = DEPTH_SPLIT * SLOTS
    slot_ids = jnp.arange(slot_total, dtype=jnp.int32)
    depth_of = slot_ids // SLOTS
    within = slot_ids % SLOTS
    live_mask = within[None, None, :] < tile_count[:, :, depth_of]
    global_rows = (jnp.arange(groups_row, dtype=jnp.int32)[:, None, None] * RB_DEV + tile_rows).reshape(groups_row * groups_col, slot_total)
    global_cols = (jnp.arange(groups_col, dtype=jnp.int32)[None, :, None] * CB_DEV + tile_cols).reshape(groups_row * groups_col, slot_total)
    flat_tiles = tiles.reshape(groups_row * groups_col, slot_total, TILE, TILE)
    flat_live = live_mask.reshape(groups_row * groups_col, slot_total)
    row_factor = jnp.ones((groups_row * RB_DEV, TILE), jnp.float32)
    col_factor = jnp.ones((groups_col * CB_DEV, TILE), jnp.float32)

    def partials(row_now, col_now, summed):

        def one_group(items):
            block_values, row_index, col_index, alive = items
            scaled = block_values * row_now[row_index][:, :, None] * col_now[col_index][:, None, :]
            magnitude = jnp.where(alive[:, None, None], jnp.abs(scaled), jnp.float32(0.0))
            if summed:
                return (magnitude.sum(axis=2), magnitude.sum(axis=1))
            return (magnitude.max(axis=2), magnitude.max(axis=1))
        row_part, col_part = lax.map(one_group, (flat_tiles, global_rows, global_cols, flat_live))
        row_zero = jnp.zeros((groups_row * RB_DEV, TILE), jnp.float32)
        col_zero = jnp.zeros((groups_col * CB_DEV, TILE), jnp.float32)
        if summed:
            row_total = row_zero.at[global_rows.reshape(-1)].add(row_part.reshape(-1, TILE))
            col_total = col_zero.at[global_cols.reshape(-1)].add(col_part.reshape(-1, TILE))
        else:
            row_total = row_zero.at[global_rows.reshape(-1)].max(row_part.reshape(-1, TILE))
            col_total = col_zero.at[global_cols.reshape(-1)].max(col_part.reshape(-1, TILE))
        return (row_total, col_total)
    for sweep_index in range(SWEEPS):
        row_peak, col_peak = partials(row_factor, col_factor, False)
        row_factor = row_factor * lax.rsqrt(row_peak + EPS)
        col_factor = col_factor * lax.rsqrt(col_peak + EPS)
    row_mass, col_mass = partials(row_factor, col_factor, True)
    row_factor = row_factor * lax.rsqrt(row_mass + EPS)
    col_factor = col_factor * lax.rsqrt(col_mass + EPS)

    def final_group(items):
        block_values, row_index, col_index, alive = items
        scaled = block_values * row_factor[row_index][:, :, None] * col_factor[col_index][:, None, :]
        return jnp.where(alive[:, None, None], scaled, jnp.float32(0.0))
    scaled_tiles = lax.map(final_group, (flat_tiles, global_rows, global_cols, flat_live))
    scaled_tiles = scaled_tiles.reshape(groups_row, groups_col, slot_total, TILE, TILE)
    return (row_factor.reshape(-1), col_factor.reshape(-1), scaled_tiles)
```

```python
import functools

import jax
import jax.numpy as jnp
from jax import lax
from jax.experimental import pallas as pl
from jax.experimental.pallas import tpu as pltpu
from jax.sharding import PartitionSpec as P

BLOCKS = 128
EPS = 1e-06
AXES = ("row", "col", "depth")
GROUP = 4
VMEM_LIMIT = 40 * 1024 * 1024


def scale_row(meta_ref, slots, t):
    return meta_ref[t], meta_ref[slots + t]


def fold(summed):
    return (lambda a, b: a + b) if summed else jnp.maximum


def tile_partials(values, row_vec, col_vec, want_row, want_col, summed):
    join = fold(summed)
    reduce = jnp.sum if summed else jnp.max
    row_halves = []
    col_acc = None
    for h in range(2):
        rows = slice(h * 128, (h + 1) * 128)
        left = jnp.abs(values[rows, 0:128])
        right = jnp.abs(values[rows, 128:256])
        if want_row:
            if col_vec is None:
                part = join(left, right)
            else:
                part = join(left * col_vec[:, 0:128], right * col_vec[:, 128:256])
            row_halves.append(reduce(part.T, axis=0, keepdims=True))
        if want_col:
            if row_vec is not None:
                factor = jnp.broadcast_to(row_vec[:, rows], (128, 128)).T
                left = left * factor
                right = right * factor
            both = [reduce(x.reshape(16, 8, 128), axis=0) for x in (left, right)]
            col_acc = both if col_acc is None else [join(a, b) for a, b in zip(col_acc, both)]
    row_out = jnp.concatenate(row_halves, axis=1) if want_row else None
    col_out = None
    if want_col:
        col_out = jnp.concatenate([reduce(a, axis=0, keepdims=True) for a in col_acc], axis=1)
    return row_out, col_out


def sweep(slots, meta_ref, tiles_ref, row_ref, col_ref, row_acc, col_acc, summed, before=None):
    want_row, want_col = row_acc is not None, col_acc is not None
    join = fold(summed)
    count = meta_ref[2 * slots]
    for acc in (row_acc, col_acc):
        if acc is not None:
            acc[...] = jnp.zeros_like(acc)

    def body(g, carry):
        found = []
        if before is not None:
            for k in range(GROUP):
                before(g * GROUP + k)
        for k in range(GROUP):
            t = g * GROUP + k
            row, col = meta_ref[t], meta_ref[slots + t]
            row_vec = None if row_ref is None else row_ref[pl.ds(row, 1), :]
            col_vec = None if col_ref is None else col_ref[pl.ds(col, 1), :]
            values = tiles_ref.at[t]
            row_out, col_out = tile_partials(values, row_vec, col_vec, want_row, want_col, summed)
            live = t < count
            if want_row:
                row_out = jnp.where(live, row_out, 0.0)
            if want_col:
                col_out = jnp.where(live, col_out, 0.0)
            found.append((row, col, row_out, col_out))
        for row, col, row_out, col_out in found:
            if want_row:
                row_acc[pl.ds(row, 1), :] = join(row_acc[pl.ds(row, 1), :], row_out)
            if want_col:
                col_acc[pl.ds(col, 1), :] = join(col_acc[pl.ds(col, 1), :], col_out)
        return carry

    lax.fori_loop(0, (count + GROUP - 1) // GROUP, body, 0)


def split(core, row_acc, col_acc, mine_ref, other_ref):
    first = core == 0
    mine_ref[...] = jnp.where(first, row_acc[...], col_acc[...])
    other_ref[...] = jnp.where(first, col_acc[...], row_acc[...])


def load_kernel(slots, meta_ref, hbm_ref, tiles_ref, mine_ref, other_ref, row_acc, col_acc, sem):
    count = meta_ref[2 * slots]

    def copy(t):
        return pltpu.make_async_copy(hbm_ref.at[t], tiles_ref.at[t], sem.at[t])

    def start(t, carry):
        copy(t).start()
        return carry

    lax.fori_loop(0, count, start, 0)

    def before(t):
        @pl.when(t < count)
        def _():
            copy(t).wait()

    sweep(slots, meta_ref, tiles_ref, None, None, row_acc, col_acc, False, before)
    split(meta_ref[2 * slots + 1], row_acc, col_acc, mine_ref, other_ref)


def row_kernel(slots, meta_ref, tiles_ref, s_ref, g_ref, part_ref, col_ref):
    first = meta_ref[2 * slots + 1] == 0
    col_ref[...] = jnp.where(first, g_ref[...], s_ref[...])
    sweep(slots, meta_ref, tiles_ref, None, col_ref, part_ref, None, False)


def col_kernel(slots, meta_ref, tiles_ref, s_ref, g_ref, part_ref, row_ref):
    first = meta_ref[2 * slots + 1] == 0
    row_ref[...] = jnp.where(first, s_ref[...], g_ref[...])
    sweep(slots, meta_ref, tiles_ref, row_ref, None, None, part_ref, False)


def both_kernel(
    slots, summed, meta_ref, tiles_ref, s_ref, g_ref, mine_ref, other_ref, row_ref, col_ref, row_acc, col_acc
):
    first = meta_ref[2 * slots + 1] == 0
    col_ref[...] = jnp.where(first, s_ref[...], g_ref[...])
    row_ref[...] = jnp.where(first, g_ref[...], s_ref[...])
    sweep(slots, meta_ref, tiles_ref, row_ref, col_ref, row_acc, col_acc, summed)
    split(meta_ref[2 * slots + 1], row_acc, col_acc, mine_ref, other_ref)


def final_kernel(slots, meta_ref, tiles_ref, row_ref, col_ref, out_ref):
    count = meta_ref[2 * slots]
    base = pl.program_id(0) * GROUP
    for k in range(GROUP):
        t = base + k

        @pl.when(t < count)
        def _():
            row_vec = row_ref[pl.ds(meta_ref[t], 1), :]
            col_vec = col_ref[pl.ds(meta_ref[slots + t], 1), :]
            for h in range(2):
                rows = slice(h * 128, (h + 1) * 128)
                factor = jnp.broadcast_to(row_vec[:, rows], (128, 128)).T
                for w in range(2):
                    cols = slice(w * 128, (w + 1) * 128)
                    out_ref[k, rows, cols] = tiles_ref[t, rows, cols] * factor * col_vec[:, cols]

        @pl.when(t >= count)
        def _():
            out_ref[k] = jnp.zeros(out_ref.shape[1:], jnp.float32)


def shards(sizes, tiles, tile_rows, tile_cols, tile_count):
    zs, xs, ys = sizes
    values = tiles[0, 0]
    slots, size = values.shape[0], values.shape[1]
    core = lax.axis_index("depth")
    is_first = core == 0
    meta = jnp.concatenate(
        [tile_rows[0, 0], tile_cols[0, 0], tile_count[0, 0], core[None].astype(jnp.int32)]
    )

    smem = pl.BlockSpec(memory_space=pltpu.SMEM)
    vmem = pl.BlockSpec(memory_space=pltpu.VMEM)
    params = pltpu.CompilerParams(vmem_limit_bytes=VMEM_LIMIT)
    vec = jax.ShapeDtypeStruct((BLOCKS, size), jnp.float32)
    acc = pltpu.VMEM((BLOCKS, size), jnp.float32)
    kept = pltpu.VMEM((slots, size, size), jnp.float32)

    def spots(move):
        pairs = []
        for z in range(zs):
            for x in range(xs):
                for y in range(ys):
                    for d in range(2):
                        to = move(z, x, y, d)
                        if to is not None:
                            pairs.append((index(z, x, y, d), index(*to)))
        return pairs

    def index(z, x, y, d):
        return ((z % zs * xs + x % xs) * ys + y % ys) * 2 + d

    steps = {
        "x": lambda z, x, y, d, s: (z, x + s, y, d),
        "y": lambda z, x, y, d, s: (z, x, y + s, d),
        "z": lambda z, x, y, d, s: (z + s, x, y, d),
    }

    def slot(v, first_axis, second_axis):
        parts = [v]
        for s in (2, 1, 3):
            def move(z, x, y, d, s=s):
                axis = first_axis if d == 0 else second_axis
                return None if axis is None else steps[axis](z, x, y, d, s)
            parts.append(lax.ppermute(v, AXES, spots(move)))
        return parts

    def top(parts):
        return jnp.maximum(jnp.maximum(parts[0], parts[1]), jnp.maximum(parts[2], parts[3]))

    def total(parts):
        return (parts[0] + parts[1]) + (parts[2] + parts[3])

    def next_factor(old, partial):
        return old * lax.rsqrt(old * partial + EPS)

    swap = lambda v: lax.ppermute(v, "depth", [(0, 1), (1, 0)])
    up = lambda v: lax.ppermute(v, "depth", [(0, 1)])
    down = lambda v: lax.ppermute(v, "depth", [(1, 0)])

    def pick(a, b):
        return jnp.where(is_first, a, b)

    held, mine, other = pl.pallas_call(
        functools.partial(load_kernel, slots),
        out_shape=(kept, vec, vec),
        in_specs=[smem, pl.BlockSpec(memory_space=pl.ANY)],
        out_specs=(vmem, vmem, vmem),
        scratch_shapes=[acc, acc, pltpu.SemaphoreType.DMA((slots,))],
        compiler_params=params,
        name="load",
    )(meta, values)
    held = pltpu.with_memory_space_constraint(held, pltpu.VMEM)

    def call(kernel, outs, scratch, name):
        def run(*args):
            return pl.pallas_call(
                kernel,
                out_shape=(vec,) * outs,
                in_specs=[smem] + [vmem] * (1 + len(args)),
                out_specs=(vmem,) * outs,
                scratch_shapes=[acc] * scratch,
                compiler_params=params,
                name=name,
            )(meta, held, *args)
        return run

    run_row = call(functools.partial(row_kernel, slots), 2, 0, "rows")
    run_col = call(functools.partial(col_kernel, slots), 2, 0, "cols")
    run_both = call(functools.partial(both_kernel, slots, False), 4, 2, "both")
    run_sums = call(functools.partial(both_kernel, slots, True), 4, 2, "sums")

    one = jnp.ones((BLOCKS, size), jnp.float32)
    row_now, col_now = one, one
    m = jnp.maximum(mine, swap(other))
    for pair in range(2):
        u = top(slot(m, "x", "z"))
        s = pick(u, next_factor(col_now, u))
        part, col_now = run_row(s, down(s))
        m = pick(s, jnp.maximum(part, up(part)))
        u = top(slot(m, "y", "x"))
        s = pick(next_factor(row_now, u), u)
        part, row_now = run_col(s, up(s))
        m = pick(jnp.maximum(part, down(part)), s)
        u = top(slot(m, "z", "y"))
        s = next_factor(pick(col_now, row_now), u)
        if pair == 0:
            mine, other, row_now, col_now = run_both(s, swap(s))
            m = jnp.maximum(mine, swap(other))
        else:
            mine, other, row_now, col_now = run_sums(s, swap(s))
            m = mine + swap(other)
    u = total(slot(m, "x", "z"))
    s = pick(u, next_factor(col_now, u))
    col_last = pick(down(s), s)
    u = total(slot(s, "y", None))
    s = next_factor(row_now, u)
    row_last = pick(s, up(s))

    scaled = pl.pallas_call(
        functools.partial(final_kernel, slots),
        out_shape=jax.ShapeDtypeStruct((slots, size, size), jnp.float32),
        grid=(slots // GROUP,),
        in_specs=[smem, vmem, vmem, vmem],
        out_specs=pl.BlockSpec((GROUP, size, size), lambda i: (i, 0, 0)),
        compiler_params=params,
        name="scaled",
    )(meta, held, row_last, col_last)
    return row_last.reshape(-1), col_last.reshape(-1), scaled[None, None]


def solution(mesh):
    zs, cs, ds = (mesh.shape[a] for a in AXES)
    xs = 4
    sizes = (zs, xs, cs // xs)
    in_specs = (
        P("row", "col", "depth", None, None),
        P("row", "col", "depth"),
        P("row", "col", "depth"),
        P("row", "col", "depth"),
    )
    out_specs = (P("row"), P("col"), P("row", "col", "depth", None, None))
    return jax.shard_map(
        functools.partial(shards, sizes), mesh=mesh, in_specs=in_specs, out_specs=out_specs, check_vma=False
    )
```

```python
import functools

import jax
import jax.numpy as jnp
from jax import lax
from jax.experimental import pallas as pl
from jax.experimental.pallas import tpu as pltpu
from jax.sharding import PartitionSpec as P

BLOCKS = 128
EPS = 1e-06
AXES = ("row", "col", "depth")
GROUP = 4
MIB = 1024 * 1024


def scale_row(meta_ref, slots, t):
    return meta_ref[t], meta_ref[slots + t]


def fold(summed):
    return (lambda a, b: a + b) if summed else jnp.maximum


def tile_partials(values, row_vec, col_vec, want_row, want_col, summed):
    join = fold(summed)
    reduce = jnp.sum if summed else jnp.max
    row_halves = []
    col_acc = None
    for h in range(2):
        rows = slice(h * 128, (h + 1) * 128)
        left = jnp.abs(values[rows, 0:128])
        right = jnp.abs(values[rows, 128:256])
        if want_row:
            if col_vec is None:
                part = join(left, right)
            else:
                part = join(left * col_vec[:, 0:128], right * col_vec[:, 128:256])
            row_halves.append(reduce(part.T, axis=0, keepdims=True))
        if want_col:
            if row_vec is not None:
                factor = jnp.broadcast_to(row_vec[:, rows], (128, 128)).T
                left = left * factor
                right = right * factor
            both = [reduce(x.reshape(16, 8, 128), axis=0) for x in (left, right)]
            col_acc = both if col_acc is None else [join(a, b) for a, b in zip(col_acc, both)]
    row_out = jnp.concatenate(row_halves, axis=1) if want_row else None
    col_out = None
    if want_col:
        col_out = jnp.concatenate([reduce(a, axis=0, keepdims=True) for a in col_acc], axis=1)
    return row_out, col_out


def sweep(slots, meta_ref, tiles_ref, row_ref, col_ref, row_acc, col_acc, summed, before=None):
    want_row, want_col = row_acc is not None, col_acc is not None
    join = fold(summed)
    count = meta_ref[2 * slots]
    for acc in (row_acc, col_acc):
        if acc is not None:
            acc[...] = jnp.zeros_like(acc)

    def body(g, carry):
        found = []
        if before is not None:
            for k in range(GROUP):
                before(g * GROUP + k)
        for k in range(GROUP):
            t = g * GROUP + k
            row, col = meta_ref[t], meta_ref[slots + t]
            row_vec = None if row_ref is None else row_ref[pl.ds(row, 1), :]
            col_vec = None if col_ref is None else col_ref[pl.ds(col, 1), :]
            values = tiles_ref.at[t]
            row_out, col_out = tile_partials(values, row_vec, col_vec, want_row, want_col, summed)
            live = t < count
            if want_row:
                row_out = jnp.where(live, row_out, 0.0)
            if want_col:
                col_out = jnp.where(live, col_out, 0.0)
            found.append((row, col, row_out, col_out))
        for row, col, row_out, col_out in found:
            if want_row:
                row_acc[pl.ds(row, 1), :] = join(row_acc[pl.ds(row, 1), :], row_out)
            if want_col:
                col_acc[pl.ds(col, 1), :] = join(col_acc[pl.ds(col, 1), :], col_out)
        return carry

    lax.fori_loop(0, (count + GROUP - 1) // GROUP, body, 0)


def split(core, row_acc, col_acc, mine_ref, other_ref):
    first = core == 0
    mine_ref[...] = jnp.where(first, row_acc[...], col_acc[...])
    other_ref[...] = jnp.where(first, col_acc[...], row_acc[...])


def load_kernel(slots, meta_ref, hbm_ref, tiles_ref, mine_ref, other_ref, first_ref, row_acc, col_acc, sem):
    count = meta_ref[2 * slots]

    def copy(t):
        return pltpu.make_async_copy(hbm_ref.at[t], tiles_ref.at[t], sem.at[t])

    def start(t, carry):
        copy(t).start()
        return carry

    lax.fori_loop(0, count, start, 0)
    first_ref[...] = jnp.where(meta_ref[2 * slots + 1] == 0, jnp.ones_like(first_ref), 0.0)

    def before(t):
        @pl.when(t < count)
        def _():
            copy(t).wait()

    sweep(slots, meta_ref, tiles_ref, None, None, row_acc, col_acc, False, before)
    split(meta_ref[2 * slots + 1], row_acc, col_acc, mine_ref, other_ref)


def row_kernel(slots, meta_ref, tiles_ref, s_ref, g_ref, part_ref, col_ref):
    first = meta_ref[2 * slots + 1] == 0
    col_ref[...] = jnp.where(first, g_ref[...], s_ref[...])
    sweep(slots, meta_ref, tiles_ref, None, col_ref, part_ref, None, False)


def col_kernel(slots, meta_ref, tiles_ref, s_ref, g_ref, part_ref, row_ref):
    first = meta_ref[2 * slots + 1] == 0
    row_ref[...] = jnp.where(first, s_ref[...], g_ref[...])
    sweep(slots, meta_ref, tiles_ref, row_ref, None, None, part_ref, False)


def both_kernel(
    slots, summed, meta_ref, tiles_ref, s_ref, g_ref, mine_ref, other_ref, row_ref, col_ref, row_acc, col_acc
):
    first = meta_ref[2 * slots + 1] == 0
    col_ref[...] = jnp.where(first, s_ref[...], g_ref[...])
    row_ref[...] = jnp.where(first, g_ref[...], s_ref[...])
    sweep(slots, meta_ref, tiles_ref, row_ref, col_ref, row_acc, col_acc, summed)
    split(meta_ref[2 * slots + 1], row_acc, col_acc, mine_ref, other_ref)


def final_kernel(slots, meta_ref, tiles_ref, row_ref, col_ref, out_ref, row_out, col_out, done, sem):
    count = meta_ref[2 * slots]
    for vec_ref, flat in ((row_ref, row_out), (col_ref, col_out)):
        for w in range(2):
            flat[pl.ds(w, BLOCKS, 2), :] = vec_ref[:, w * 128 : (w + 1) * 128]

    def copy(t):
        return pltpu.make_async_copy(done.at[t], out_ref.at[t], sem.at[t])

    def zero(t, carry):
        done[t] = jnp.zeros(done.shape[1:], jnp.float32)
        copy(t).start()
        return carry

    lax.fori_loop(count, slots, zero, 0)

    def fill(t, carry):
        row_vec = row_ref[pl.ds(meta_ref[t], 1), :]
        col_vec = col_ref[pl.ds(meta_ref[slots + t], 1), :]
        for h in range(2):
            rows = slice(h * 128, (h + 1) * 128)
            factor = jnp.broadcast_to(row_vec[:, rows], (128, 128)).T
            for w in range(2):
                cols = slice(w * 128, (w + 1) * 128)
                done[t, rows, cols] = tiles_ref[t, rows, cols] * factor * col_vec[:, cols]
        copy(t).start()
        return carry

    lax.fori_loop(0, count, fill, 0)

    def finish(t, carry):
        copy(t).wait()
        return carry

    lax.fori_loop(0, slots, finish, 0)


def shards(sizes, tiles, tile_rows, tile_cols, tile_count):
    zs, xs, ys = sizes
    values = tiles[0, 0]
    slots, size = values.shape[0], values.shape[1]
    core = lax.axis_index("depth")
    meta = jnp.concatenate(
        [tile_rows[0, 0], tile_cols[0, 0], tile_count[0, 0], core[None].astype(jnp.int32)]
    )

    smem = pl.BlockSpec(memory_space=pltpu.SMEM)
    vmem = pl.BlockSpec(memory_space=pltpu.VMEM)
    params = pltpu.CompilerParams(vmem_limit_bytes=8 * MIB)
    vec = jax.ShapeDtypeStruct((BLOCKS, size), jnp.float32)
    acc = pltpu.VMEM((BLOCKS, size), jnp.float32)
    kept = pltpu.VMEM((slots, size, size), jnp.float32)

    def spots(move):
        pairs = []
        for z in range(zs):
            for x in range(xs):
                for y in range(ys):
                    for d in range(2):
                        pairs.append((index(z, x, y, d), index(*move(z, x, y, d))))
        return pairs

    def index(z, x, y, d):
        return ((z * xs + x) * ys + y) * 2 + d

    steps = {
        "x": lambda z, x, y, d, s: (z, x ^ s, y, d),
        "y": lambda z, x, y, d, s: (z, x, y ^ s, d),
        "z": lambda z, x, y, d, s: (z ^ s, x, y, d),
    }

    def slot(v, first_axis, second_axis):
        parts = [v]
        for s in (2, 1, 3):
            def move(z, x, y, d, s=s):
                return steps[first_axis if d == 0 else second_axis](z, x, y, d, s)
            parts.append(lax.ppermute(v, AXES, spots(move)))
        return parts

    def top(parts):
        return jnp.maximum(jnp.maximum(parts[0], parts[1]), jnp.maximum(parts[2], parts[3]))

    def total(parts):
        return (parts[0] + parts[1]) + (parts[2] + parts[3])

    def next_factor(old, partial):
        return old * lax.rsqrt(old * partial + EPS)

    swap = lambda v: lax.ppermute(v, "depth", [(0, 1), (1, 0)])

    def pick(a, b):
        return jnp.where(is_first > 0.5, a, b)

    held, mine, other, is_first = pl.pallas_call(
        functools.partial(load_kernel, slots),
        out_shape=(kept, vec, vec, vec),
        in_specs=[smem, pl.BlockSpec(memory_space=pltpu.HBM)],
        out_specs=(vmem, vmem, vmem, vmem),
        scratch_shapes=[acc, acc, pltpu.SemaphoreType.DMA((slots,))],
        compiler_params=params,
        name="load",
    )(meta, pltpu.with_memory_space_constraint(values, pltpu.HBM))
    held = pltpu.with_memory_space_constraint(held, pltpu.VMEM)

    def call(kernel, outs, scratch, name):
        def run(*args):
            return pl.pallas_call(
                kernel,
                out_shape=(vec,) * outs,
                in_specs=[smem] + [vmem] * (1 + len(args)),
                out_specs=(vmem,) * outs,
                scratch_shapes=[acc] * scratch,
                compiler_params=params,
                name=name,
            )(meta, held, *args)
        return run

    run_row = call(functools.partial(row_kernel, slots), 2, 0, "rows")
    run_col = call(functools.partial(col_kernel, slots), 2, 0, "cols")
    run_both = call(functools.partial(both_kernel, slots, False), 4, 2, "both")
    run_sums = call(functools.partial(both_kernel, slots, True), 4, 2, "sums")

    one = jnp.ones((BLOCKS, size), jnp.float32)
    row_now, col_now = one, one
    m = jnp.maximum(mine, swap(other))
    for pair in range(2):
        u = top(slot(m, "x", "z"))
        s = pick(u, next_factor(col_now, u))
        part, col_now = run_row(s, swap(s))
        m = pick(s, jnp.maximum(part, swap(part)))
        u = top(slot(m, "y", "x"))
        s = pick(next_factor(row_now, u), u)
        part, row_now = run_col(s, swap(s))
        m = pick(jnp.maximum(part, swap(part)), s)
        u = top(slot(m, "z", "y"))
        s = next_factor(pick(col_now, row_now), u)
        if pair == 0:
            mine, other, row_now, col_now = run_both(s, swap(s))
            m = jnp.maximum(mine, swap(other))
        else:
            mine, other, row_now, col_now = run_sums(s, swap(s))
            m = mine + swap(other)
    u = total(slot(m, "x", "z"))
    s = pick(u, next_factor(col_now, u))
    col_last = pick(swap(s), s)
    u = total(slot(s, "y", "x"))
    s = next_factor(row_now, u)
    row_last = pick(s, swap(s))

    flat = jax.ShapeDtypeStruct((2 * BLOCKS, size // 2), jnp.float32)
    scaled, row_out, col_out = pl.pallas_call(
        functools.partial(final_kernel, slots),
        out_shape=(jax.ShapeDtypeStruct((slots, size, size), jnp.float32), flat, flat),
        in_specs=[smem, vmem, vmem, vmem],
        out_specs=(pl.BlockSpec(memory_space=pltpu.HBM), vmem, vmem),
        scratch_shapes=[pltpu.VMEM((slots, size, size), jnp.float32), pltpu.SemaphoreType.DMA((slots,))],
        compiler_params=pltpu.CompilerParams(vmem_limit_bytes=16 * MIB),
        name="scaled",
    )(meta, held, row_last, col_last)
    return row_out.reshape(-1), col_out.reshape(-1), scaled[None, None]


def solution(mesh):
    zs, cs, ds = (mesh.shape[a] for a in AXES)
    xs = 4
    sizes = (zs, xs, cs // xs)
    in_specs = (
        P("row", "col", "depth", None, None),
        P("row", "col", "depth"),
        P("row", "col", "depth"),
        P("row", "col", "depth"),
    )
    out_specs = (P("row"), P("col"), P("row", "col", "depth", None, None))
    return jax.shard_map(
        functools.partial(shards, sizes), mesh=mesh, in_specs=in_specs, out_specs=out_specs, check_vma=False
    )
```

```python
import functools
import math

import jax
import jax.numpy as jnp
from jax import lax
from jax.experimental import pallas as pl
from jax.experimental.pallas import tpu as pltpu
from jax.sharding import PartitionSpec as P

BLOCKS = 128
EPS = 1e-06
AXES = ("row", "col", "depth")
LOAD_GROUP = 8
SWEEP_GROUP = 12
FINAL_GROUP = 4
MIB = 1024 * 1024


def scale_row(meta_ref, slots, t):
    return meta_ref[t], meta_ref[slots + t]


def fold(summed):
    return (lambda a, b: a + b) if summed else jnp.maximum


def tile_partials(values, row_vec, col_vec, want_row, want_col, summed):
    join = fold(summed)
    reduce = jnp.sum if summed else jnp.max
    row_halves = []
    col_acc = None
    for h in range(2):
        rows = slice(h * 128, (h + 1) * 128)
        left = jnp.abs(values[rows, 0:128])
        right = jnp.abs(values[rows, 128:256])
        if want_row:
            if col_vec is None:
                part = join(left, right)
            else:
                part = join(left * col_vec[:, 0:128], right * col_vec[:, 128:256])
            row_halves.append(reduce(part.T, axis=0, keepdims=True))
        if want_col:
            if row_vec is not None:
                factor = jnp.broadcast_to(row_vec[:, rows], (128, 128)).T
                left = left * factor
                right = right * factor
            both = [reduce(x.reshape(16, 8, 128), axis=0) for x in (left, right)]
            col_acc = both if col_acc is None else [join(a, b) for a, b in zip(col_acc, both)]
    row_out = jnp.concatenate(row_halves, axis=1) if want_row else None
    col_out = None
    if want_col:
        col_out = jnp.concatenate([reduce(a, axis=0, keepdims=True) for a in col_acc], axis=1)
    return row_out, col_out


def clear(*accs):
    for acc in accs:
        if acc is not None:
            acc[...] = jnp.zeros_like(acc)


def sweep(slots, group, meta_ref, tiles_ref, offset, row_ref, col_ref, row_acc, col_acc, summed, before=None):
    want_row, want_col = row_acc is not None, col_acc is not None
    join = fold(summed)
    held = tiles_ref.shape[0]
    group = math.gcd(held, group)
    count = jnp.clip(meta_ref[2 * slots] - offset, 0, held)

    def body(g, carry):
        found = []
        if before is not None:
            for k in range(group):
                before(g * group + k)
        for k in range(group):
            t = g * group + k
            row, col = meta_ref[offset + t], meta_ref[slots + offset + t]
            row_vec = None if row_ref is None else row_ref[pl.ds(row, 1), :]
            col_vec = None if col_ref is None else col_ref[pl.ds(col, 1), :]
            values = tiles_ref.at[t]
            row_out, col_out = tile_partials(values, row_vec, col_vec, want_row, want_col, summed)
            live = t < count
            if want_row:
                row_out = jnp.where(live, row_out, 0.0)
            if want_col:
                col_out = jnp.where(live, col_out, 0.0)
            found.append((row, col, row_out, col_out))
        for row, col, row_out, col_out in found:
            if want_row:
                row_acc[pl.ds(row, 1), :] = join(row_acc[pl.ds(row, 1), :], row_out)
            if want_col:
                col_acc[pl.ds(col, 1), :] = join(col_acc[pl.ds(col, 1), :], col_out)
        return carry

    lax.fori_loop(0, (count + group - 1) // group, body, 0)


def split(core, row_acc, col_acc, mine_ref, other_ref):
    first = core == 0
    mine_ref[...] = jnp.where(first, row_acc[...], col_acc[...])
    other_ref[...] = jnp.where(first, col_acc[...], row_acc[...])


def load_kernel(
    slots, half, meta_ref, hbm_ref, low_ref, high_ref, mine_ref, other_ref, first_ref, row_acc, col_acc, sem
):
    count = meta_ref[2 * slots]
    pieces = ((low_ref, 0), (high_ref, half))

    def copy(ref, offset, t):
        return pltpu.make_async_copy(hbm_ref.at[offset + t], ref.at[t], sem.at[offset + t])

    for ref, offset in pieces:

        def start(t, carry, ref=ref, offset=offset):
            copy(ref, offset, t).start()
            return carry

        lax.fori_loop(0, jnp.clip(count - offset, 0, half), start, 0)
    first_ref[...] = jnp.where(meta_ref[2 * slots + 1] == 0, jnp.ones_like(first_ref), 0.0)
    clear(row_acc, col_acc)
    for ref, offset in pieces:

        def before(t, ref=ref, offset=offset):
            @pl.when(t + offset < count)
            def _():
                copy(ref, offset, t).wait()

        sweep(slots, LOAD_GROUP, meta_ref, ref, offset, None, None, row_acc, col_acc, False, before)
    split(meta_ref[2 * slots + 1], row_acc, col_acc, mine_ref, other_ref)


def row_kernel(slots, half, meta_ref, low_ref, high_ref, s_ref, g_ref, part_ref, col_ref):
    first = meta_ref[2 * slots + 1] == 0
    col_ref[...] = jnp.where(first, g_ref[...], s_ref[...])
    clear(part_ref)
    for ref, offset in ((low_ref, 0), (high_ref, half)):
        sweep(slots, SWEEP_GROUP, meta_ref, ref, offset, None, col_ref, part_ref, None, False)


def col_kernel(slots, half, meta_ref, low_ref, high_ref, s_ref, g_ref, part_ref, row_ref):
    first = meta_ref[2 * slots + 1] == 0
    row_ref[...] = jnp.where(first, s_ref[...], g_ref[...])
    clear(part_ref)
    for ref, offset in ((low_ref, 0), (high_ref, half)):
        sweep(slots, SWEEP_GROUP, meta_ref, ref, offset, row_ref, None, None, part_ref, False)


def chip_kernel(
    slots, half, kinds, summed, meta_ref, twin_ref, low_ref, high_ref, twin_low_ref, twin_high_ref, s_ref, part_ref
):
    core = meta_ref[2 * slots + 1]
    pieces = (
        (meta_ref, low_ref, 0),
        (meta_ref, high_ref, half),
        (twin_ref, twin_low_ref, 0),
        (twin_ref, twin_high_ref, half),
    )
    for place, kind in enumerate(kinds):

        @pl.when(core == place)
        def _():
            if kind is None:
                part_ref[...] = s_ref[...]
                return
            clear(part_ref)
            for meta, ref, offset in pieces:
                if kind == "rows":
                    sweep(slots, SWEEP_GROUP, meta, ref, offset, None, s_ref, part_ref, None, summed)
                else:
                    sweep(slots, SWEEP_GROUP, meta, ref, offset, s_ref, None, None, part_ref, summed)


def final_kernel(slots, half, meta_ref, low_ref, high_ref, row_ref, col_ref, out_ref, row_out, col_out, done, sem):
    count = meta_ref[2 * slots]
    group = math.gcd(half, FINAL_GROUP)

    def copy(t):
        return pltpu.make_async_copy(done.at[t], out_ref.at[t], sem.at[t])

    for ref, offset in ((low_ref, 0), (high_ref, half)):

        def fill(g, carry, ref=ref, offset=offset):
            for k in range(group):
                t = g * group + k
                slot = offset + t
                live = slot < count
                row_vec = row_ref[pl.ds(meta_ref[slot], 1), :]
                col_vec = col_ref[pl.ds(meta_ref[slots + slot], 1), :]
                for h in range(2):
                    rows = slice(h * 128, (h + 1) * 128)
                    factor = jnp.broadcast_to(row_vec[:, rows], (128, 128)).T
                    for w in range(2):
                        cols = slice(w * 128, (w + 1) * 128)
                        scaled = ref[t, rows, cols] * factor * col_vec[:, cols]
                        done[slot, rows, cols] = jnp.where(live, scaled, 0.0)
            for k in range(group):
                copy(offset + g * group + k).start()
            return carry

        full = (jnp.clip(count - offset, 0, half) + group - 1) // group
        lax.fori_loop(0, full, fill, 0)

        def zero(slot, carry):
            done[slot] = jnp.zeros(done.shape[1:], jnp.float32)
            copy(slot).start()
            return carry

        lax.fori_loop(offset + full * group, offset + half, zero, 0)
    for vec_ref, flat in ((row_ref, row_out), (col_ref, col_out)):
        for w in range(2):
            flat[pl.ds(w, BLOCKS, 2), :] = vec_ref[:, w * 128 : (w + 1) * 128]

    def finish(t, carry):
        copy(t).wait()
        return carry

    lax.fori_loop(0, slots, finish, 0)


def shards(sizes, tiles, tile_rows, tile_cols, tile_count):
    zs, xs, ys = sizes
    values = tiles[0, 0]
    slots, size = values.shape[0], values.shape[1]
    core = lax.axis_index("depth")
    meta = jnp.concatenate(
        [tile_rows[0, 0], tile_cols[0, 0], tile_count[0, 0], core[None].astype(jnp.int32)]
    )

    smem = pl.BlockSpec(memory_space=pltpu.SMEM)
    vmem = pl.BlockSpec(memory_space=pltpu.VMEM)
    params = pltpu.CompilerParams(vmem_limit_bytes=8 * MIB)
    vec = jax.ShapeDtypeStruct((BLOCKS, size), jnp.float32)
    acc = pltpu.VMEM((BLOCKS, size), jnp.float32)
    half = slots // 2
    kept = pltpu.VMEM((half, size, size), jnp.float32)

    def spots(move):
        pairs = []
        for z in range(zs):
            for x in range(xs):
                for y in range(ys):
                    for d in range(2):
                        pairs.append((index(z, x, y, d), index(*move(z, x, y, d))))
        return pairs

    def index(z, x, y, d):
        return ((z * xs + x) * ys + y) * 2 + d

    steps = {
        "x": lambda z, x, y, d, s: (z, x ^ s, y, d),
        "y": lambda z, x, y, d, s: (z, x, y ^ s, d),
        "z": lambda z, x, y, d, s: (z ^ s, x, y, d),
    }

    def slot(v, first_axis, second_axis):
        parts = [v]
        for s in (2, 1, 3):
            def move(z, x, y, d, s=s):
                return steps[first_axis if d == 0 else second_axis](z, x, y, d, s)
            parts.append(lax.ppermute(v, AXES, spots(move)))
        return parts

    def top(parts):
        return jnp.maximum(jnp.maximum(parts[0], parts[1]), jnp.maximum(parts[2], parts[3]))

    def total(parts):
        return (parts[0] + parts[1]) + (parts[2] + parts[3])

    def next_factor(old, partial):
        return old * lax.rsqrt(old * partial + EPS)

    swap = lambda v: lax.ppermute(v, "depth", [(0, 1), (1, 0)])

    def pick(a, b):
        return jnp.where(is_first > 0.5, a, b)

    low, high, mine, other, is_first = pl.pallas_call(
        functools.partial(load_kernel, slots, half),
        out_shape=(kept, kept, vec, vec, vec),
        in_specs=[smem, pl.BlockSpec(memory_space=pltpu.HBM)],
        out_specs=(vmem,) * 5,
        scratch_shapes=[acc, acc, pltpu.SemaphoreType.DMA((slots,))],
        compiler_params=params,
        name="load",
    )(meta, pltpu.with_memory_space_constraint(values, pltpu.HBM))

    def stay(v):
        return pltpu.with_memory_space_constraint(v, pltpu.VMEM)

    def share(v, after):
        v, after = lax.optimization_barrier((v, after))
        return swap(v), after

    def own(kernel, name):
        def run(*args):
            return pl.pallas_call(
                functools.partial(kernel, slots, half),
                out_shape=(vec, vec),
                in_specs=[smem] + [vmem] * 4,
                out_specs=(vmem, vmem),
                compiler_params=params,
                name=name,
            )(meta, stay(low), stay(high), *args)
        return run

    def chip(kinds, summed, name, s):
        return pl.pallas_call(
            functools.partial(chip_kernel, slots, half, kinds, summed),
            out_shape=vec,
            in_specs=[smem, smem] + [vmem] * 5,
            out_specs=vmem,
            compiler_params=params,
            name=name,
        )(meta, twin, stay(low), stay(high), stay(twin_low), stay(twin_high), s)

    def late_swap(v, parts):
        return swap(lax.optimization_barrier((v, parts[1]))[0])

    twin = swap(meta)
    m = jnp.maximum(mine, swap(other))
    twin_low, m = share(low, m)
    u = top(slot(m, "x", "z"))
    s = pick(u, lax.rsqrt(u + EPS))
    twin_low, s = lax.optimization_barrier((twin_low, s))
    part, col_1 = own(row_kernel, "rows")(s, swap(s))
    m = pick(s, jnp.maximum(part, swap(part)))
    twin_high, m = share(high, m)
    u = top(slot(m, "y", "x"))
    s = pick(lax.rsqrt(u + EPS), u)
    twin_high, s = lax.optimization_barrier((twin_high, s))
    part, row_1 = own(col_kernel, "cols")(s, swap(s))
    m = pick(jnp.maximum(part, swap(part)), s)
    u = top(slot(m, "z", "y"))
    now_2 = next_factor(pick(col_1, row_1), u)

    parts = slot(chip(("rows", "cols"), False, "chip_both", now_2), "x", "z")
    old_2 = late_swap(now_2, parts)
    u = top(parts)
    s = pick(u, next_factor(old_2, u))
    col_3 = swap(s)
    u = top(slot(chip((None, "rows"), False, "chip_rows", s), "y", "x"))
    s = pick(next_factor(old_2, u), u)
    row_3 = swap(s)
    u = top(slot(chip(("cols", None), False, "chip_cols", s), "z", "y"))
    now_4 = next_factor(pick(col_3, row_3), u)
    parts = slot(chip(("rows", "cols"), True, "chip_sums", now_4), "x", "z")
    old_4 = late_swap(now_4, parts)
    u = total(parts)
    s = pick(u, next_factor(old_4, u))
    col_last = pick(swap(s), s)
    u = total(slot(s, "y", "x"))
    s = next_factor(old_4, u)
    row_last = pick(s, swap(s))

    flat = jax.ShapeDtypeStruct((2 * BLOCKS, size // 2), jnp.float32)
    scaled, row_out, col_out = pl.pallas_call(
        functools.partial(final_kernel, slots, half),
        out_shape=(jax.ShapeDtypeStruct((slots, size, size), jnp.float32), flat, flat),
        in_specs=[smem] + [vmem] * 4,
        out_specs=(pl.BlockSpec(memory_space=pltpu.HBM), vmem, vmem),
        scratch_shapes=[pltpu.VMEM((slots, size, size), jnp.float32), pltpu.SemaphoreType.DMA((slots,))],
        compiler_params=pltpu.CompilerParams(vmem_limit_bytes=16 * MIB),
        name="scaled",
    )(meta, stay(low), stay(high), row_last, col_last)
    return row_out.reshape(-1), col_out.reshape(-1), scaled[None, None]


def solution(mesh):
    zs, cs, ds = (mesh.shape[a] for a in AXES)
    xs = 4
    sizes = (zs, xs, cs // xs)
    in_specs = (
        P("row", "col", "depth", None, None),
        P("row", "col", "depth"),
        P("row", "col", "depth"),
        P("row", "col", "depth"),
    )
    out_specs = (P("row"), P("col"), P("row", "col", "depth", None, None))
    return jax.shard_map(
        functools.partial(shards, sizes), mesh=mesh, in_specs=in_specs, out_specs=out_specs, check_vma=False
    )
```

```python
import functools
import math

import jax
import jax.numpy as jnp
from jax import lax
from jax.experimental import pallas as pl
from jax.experimental.pallas import tpu as pltpu
from jax.sharding import PartitionSpec as P

BLOCKS = 128
EPS = 1e-06
AXES = ("row", "col", "depth")
LOAD_GROUP = 8
SWEEP_GROUP = 16
CHIP_GROUP = 8
COPY_GROUP = 4
PIECES = 3
ORDER = (1, 3, 2)
MIB = 1024 * 1024


def scale_row(meta_ref, slots, t):
    return meta_ref[t], meta_ref[slots + t]


def fold(summed):
    return (lambda a, b: a + b) if summed else jnp.maximum


def tile_partials(values, row_vec, col_vec, want_row, want_col, summed):
    join = fold(summed)
    reduce = jnp.sum if summed else jnp.max
    row_halves = []
    col_acc = None
    for h in range(2):
        rows = slice(h * 128, (h + 1) * 128)
        left = jnp.abs(values[rows, 0:128])
        right = jnp.abs(values[rows, 128:256])
        if want_row:
            if col_vec is None:
                part = join(left, right)
            else:
                part = join(left * col_vec[:, 0:128], right * col_vec[:, 128:256])
            row_halves.append(reduce(part.T, axis=0, keepdims=True))
        if want_col:
            if row_vec is not None:
                factor = jnp.broadcast_to(row_vec[:, rows], (128, 128)).T
                left = left * factor
                right = right * factor
            both = [reduce(x.reshape(16, 8, 128), axis=0) for x in (left, right)]
            col_acc = both if col_acc is None else [join(a, b) for a, b in zip(col_acc, both)]
    row_out = jnp.concatenate(row_halves, axis=1) if want_row else None
    col_out = None
    if want_col:
        col_out = jnp.concatenate([reduce(a, axis=0, keepdims=True) for a in col_acc], axis=1)
    return row_out, col_out


def clear(*accs):
    for acc in accs:
        if acc is not None:
            acc[...] = jnp.zeros_like(acc)


def sweep(slots, group, meta_ref, tiles_ref, offset, row_ref, col_ref, row_acc, col_acc, summed, before=None, step=1):
    want_row, want_col = row_acc is not None, col_acc is not None
    join = fold(summed)
    held = tiles_ref.shape[0]
    group = math.gcd(held, group)
    count = jnp.clip(meta_ref[2 * slots] - offset, 0, held)

    def body(g, carry):
        found = []
        if before is not None:
            for k in range(0, group, step):
                before(g * group + k)
        for k in range(group):
            t = g * group + k
            row, col = meta_ref[offset + t], meta_ref[slots + offset + t]
            row_vec = None if row_ref is None else row_ref[pl.ds(row, 1), :]
            col_vec = None if col_ref is None else col_ref[pl.ds(col, 1), :]
            values = tiles_ref.at[t]
            row_out, col_out = tile_partials(values, row_vec, col_vec, want_row, want_col, summed)
            live = t < count
            if want_row:
                row_out = jnp.where(live, row_out, 0.0)
            if want_col:
                col_out = jnp.where(live, col_out, 0.0)
            found.append((row, col, row_out, col_out))
        for row, col, row_out, col_out in found:
            if want_row:
                row_acc[pl.ds(row, 1), :] = join(row_acc[pl.ds(row, 1), :], row_out)
            if want_col:
                col_acc[pl.ds(col, 1), :] = join(col_acc[pl.ds(col, 1), :], col_out)
        return carry

    lax.fori_loop(0, (count + group - 1) // group, body, 0)


def split(core, row_acc, col_acc, mine_ref, other_ref):
    first = core == 0
    mine_ref[...] = jnp.where(first, row_acc[...], col_acc[...])
    other_ref[...] = jnp.where(first, col_acc[...], row_acc[...])


def load_kernel(slots, size, meta_ref, hbm_ref, *refs):
    held, (mine_ref, other_ref, first_ref, row_acc, col_acc, sem) = refs[:PIECES], refs[PIECES:]
    count = meta_ref[2 * slots]
    step = math.gcd(size, COPY_GROUP)
    group = math.gcd(size, LOAD_GROUP)

    def copy(ref, offset, g):
        return pltpu.make_async_copy(
            hbm_ref.at[pl.ds(offset + g * step, step)], ref.at[pl.ds(g * step, step)], sem.at[offset // step + g]
        )

    for place, ref in enumerate(held):

        def start(g, carry, ref=ref, offset=place * size):
            copy(ref, offset, g).start()
            return carry

        lax.fori_loop(0, (jnp.clip(count - place * size, 0, size) + step - 1) // step, start, 0)
    first_ref[...] = jnp.where(meta_ref[2 * slots + 1] == 0, jnp.ones_like(first_ref), 0.0)
    clear(row_acc, col_acc)
    for place, ref in enumerate(held):

        def before(t, ref=ref, offset=place * size):
            @pl.when(offset + t < count)
            def _():
                copy(ref, offset, t // step).wait()

        sweep(slots, group, meta_ref, ref, place * size, None, None, row_acc, col_acc, False, before, step)
    split(meta_ref[2 * slots + 1], row_acc, col_acc, mine_ref, other_ref)


def row_kernel(slots, size, meta_ref, *refs):
    held, (s_ref, g_ref, part_ref, col_ref) = refs[:PIECES], refs[PIECES:]
    first = meta_ref[2 * slots + 1] == 0
    col_ref[...] = jnp.where(first, g_ref[...], s_ref[...])
    clear(part_ref)
    for place, ref in enumerate(held):
        sweep(slots, SWEEP_GROUP, meta_ref, ref, place * size, None, col_ref, part_ref, None, False)


def col_kernel(slots, size, meta_ref, *refs):
    held, (s_ref, g_ref, part_ref, row_ref) = refs[:PIECES], refs[PIECES:]
    first = meta_ref[2 * slots + 1] == 0
    row_ref[...] = jnp.where(first, s_ref[...], g_ref[...])
    clear(part_ref)
    for place, ref in enumerate(held):
        sweep(slots, SWEEP_GROUP, meta_ref, ref, place * size, row_ref, None, None, part_ref, False)


def chip_kernel(slots, size, kinds, summed, meta_ref, twin_ref, *refs):
    held, twins, (s_ref, part_ref) = refs[:PIECES], refs[PIECES : 2 * PIECES], refs[2 * PIECES :]
    core = meta_ref[2 * slots + 1]
    for place, kind in enumerate(kinds):

        @pl.when(core == place)
        def _():
            if kind is None:
                part_ref[...] = s_ref[...]
                return
            clear(part_ref)
            for meta, pieces in ((meta_ref, held), (twin_ref, twins)):
                for spot, ref in enumerate(pieces):
                    if kind == "rows":
                        sweep(slots, CHIP_GROUP, meta, ref, spot * size, None, s_ref, part_ref, None, summed)
                    else:
                        sweep(slots, CHIP_GROUP, meta, ref, spot * size, s_ref, None, None, part_ref, summed)


def final_kernel(slots, size, meta_ref, *refs):
    held, (row_ref, col_ref, out_ref, row_out, col_out, done, sem) = refs[:PIECES], refs[PIECES:]
    count = meta_ref[2 * slots]
    group = math.gcd(size, COPY_GROUP)

    def copy(g):
        span = pl.ds(g * group, group)
        return pltpu.make_async_copy(done.at[span], out_ref.at[span], sem.at[g])

    for place, ref in enumerate(held):
        offset = place * size

        def fill(g, carry, ref=ref, offset=offset):
            for k in range(group):
                t = g * group + k
                slot = offset + t
                live = slot < count
                row_vec = row_ref[pl.ds(meta_ref[slot], 1), :]
                col_vec = col_ref[pl.ds(meta_ref[slots + slot], 1), :]
                for h in range(2):
                    rows = slice(h * 128, (h + 1) * 128)
                    factor = jnp.broadcast_to(row_vec[:, rows], (128, 128)).T
                    for w in range(2):
                        cols = slice(w * 128, (w + 1) * 128)
                        scaled = ref[t, rows, cols] * factor * col_vec[:, cols]
                        done[slot, rows, cols] = jnp.where(live, scaled, 0.0)
            copy(offset // group + g).start()
            return carry

        full = (jnp.clip(count - offset, 0, size) + group - 1) // group
        lax.fori_loop(0, full, fill, 0)

        def zero(g, carry, offset=offset):
            done[pl.ds(offset + g * group, group)] = jnp.zeros((group,) + done.shape[1:], jnp.float32)
            copy(offset // group + g).start()
            return carry

        lax.fori_loop(full, size // group, zero, 0)
    for vec_ref, flat in ((row_ref, row_out), (col_ref, col_out)):
        for w in range(2):
            flat[pl.ds(w, BLOCKS, 2), :] = vec_ref[:, w * 128 : (w + 1) * 128]

    def finish(g, carry):
        copy(g).wait()
        return carry

    lax.fori_loop(0, slots // group, finish, 0)


def shards(sizes, tiles, tile_rows, tile_cols, tile_count):
    zs, xs, ys = sizes
    values = tiles[0, 0]
    slots, size = values.shape[0], values.shape[1]
    core = lax.axis_index("depth")
    meta = jnp.concatenate(
        [tile_rows[0, 0], tile_cols[0, 0], tile_count[0, 0], core[None].astype(jnp.int32)]
    )

    smem = pl.BlockSpec(memory_space=pltpu.SMEM)
    vmem = pl.BlockSpec(memory_space=pltpu.VMEM)
    params = pltpu.CompilerParams(vmem_limit_bytes=8 * MIB)
    vec = jax.ShapeDtypeStruct((BLOCKS, size), jnp.float32)
    acc = pltpu.VMEM((BLOCKS, size), jnp.float32)
    part_slots = slots // PIECES
    kept = pltpu.VMEM((part_slots, size, size), jnp.float32)

    def spots(move):
        pairs = []
        for z in range(zs):
            for x in range(xs):
                for y in range(ys):
                    for d in range(2):
                        pairs.append((index(z, x, y, d), index(*move(z, x, y, d))))
        return pairs

    def index(z, x, y, d):
        return ((z * xs + x) * ys + y) * 2 + d

    steps = {
        "x": lambda z, x, y, d, s: (z, x ^ s, y, d),
        "y": lambda z, x, y, d, s: (z, x, y ^ s, d),
        "z": lambda z, x, y, d, s: (z ^ s, x, y, d),
    }

    def slot(v, first_axis, second_axis):
        parts = [v]
        for s in ORDER:
            def move(z, x, y, d, s=s):
                return steps[first_axis if d == 0 else second_axis](z, x, y, d, s)
            parts.append(lax.ppermute(v, AXES, spots(move)))
        return parts

    def top(parts):
        return jnp.maximum(jnp.maximum(parts[0], parts[1]), jnp.maximum(parts[2], parts[3]))

    def total(parts):
        return (parts[0] + parts[1]) + (parts[2] + parts[3])

    def next_factor(old, partial):
        return old * lax.rsqrt(old * partial + EPS)

    swap = lambda v: lax.ppermute(v, "depth", [(0, 1), (1, 0)])

    def pick(a, b):
        return jnp.where(is_first > 0.5, a, b)

    *held, mine, other, is_first = pl.pallas_call(
        functools.partial(load_kernel, slots, part_slots),
        out_shape=(kept,) * PIECES + (vec, vec, vec),
        in_specs=[smem, pl.BlockSpec(memory_space=pltpu.HBM)],
        out_specs=(vmem,) * (PIECES + 3),
        scratch_shapes=[acc, acc, pltpu.SemaphoreType.DMA((slots,))],
        compiler_params=params,
        name="load",
    )(meta, pltpu.with_memory_space_constraint(values, pltpu.HBM))

    def stay(pieces):
        return [pltpu.with_memory_space_constraint(v, pltpu.VMEM) for v in pieces]

    twins = []

    def share(after):
        v, after = lax.optimization_barrier((held[len(twins)], after))
        twins.append(swap(v))
        return after

    def shared(before):
        twins[-1], before = lax.optimization_barrier((twins[-1], before))
        return before

    def own(kernel, name):
        def run(*args):
            return pl.pallas_call(
                functools.partial(kernel, slots, part_slots),
                out_shape=(vec, vec),
                in_specs=[smem] + [vmem] * (PIECES + 2),
                out_specs=(vmem, vmem),
                compiler_params=params,
                name=name,
            )(meta, *stay(held), *args)
        return run

    def chip(kinds, summed, name, s):
        return pl.pallas_call(
            functools.partial(chip_kernel, slots, part_slots, kinds, summed),
            out_shape=vec,
            in_specs=[smem, smem] + [vmem] * (2 * PIECES + 1),
            out_specs=vmem,
            compiler_params=params,
            name=name,
        )(meta, twin, *stay(held), *stay(twins), s)

    def late_swap(v, parts):
        return swap(lax.optimization_barrier((v, parts[1]))[0])

    twin = swap(meta)
    m = jnp.maximum(mine, swap(other))
    m = share(m)
    u = top(slot(m, "x", "z"))
    s = pick(u, lax.rsqrt(u + EPS))
    s = shared(s)
    part, col_1 = own(row_kernel, "rows")(s, swap(s))
    m = pick(s, jnp.maximum(part, swap(part)))
    m = share(m)
    u = top(slot(m, "y", "x"))
    s = pick(lax.rsqrt(u + EPS), u)
    s = shared(s)
    part, row_1 = own(col_kernel, "cols")(s, swap(s))
    m = share(pick(jnp.maximum(part, swap(part)), s))
    u = top(slot(m, "z", "y"))
    now_2 = next_factor(pick(col_1, row_1), u)

    parts = slot(chip(("rows", "cols"), False, "chip_both", now_2), "x", "z")
    old_2 = late_swap(now_2, parts)
    u = top(parts)
    s = pick(u, next_factor(old_2, u))
    col_3 = swap(s)
    u = top(slot(chip((None, "rows"), False, "chip_rows", s), "y", "x"))
    s = pick(next_factor(old_2, u), u)
    row_3 = swap(s)
    u = top(slot(chip(("cols", None), False, "chip_cols", s), "z", "y"))
    now_4 = next_factor(pick(col_3, row_3), u)
    parts = slot(chip(("rows", "cols"), True, "chip_sums", now_4), "x", "z")
    old_4 = late_swap(now_4, parts)
    u = total(parts)
    s = pick(u, next_factor(old_4, u))
    col_last = pick(swap(s), s)
    u = total(slot(s, "y", "x"))
    s = next_factor(old_4, u)
    row_last = pick(s, swap(s))

    flat = jax.ShapeDtypeStruct((2 * BLOCKS, size // 2), jnp.float32)
    scaled, row_out, col_out = pl.pallas_call(
        functools.partial(final_kernel, slots, part_slots),
        out_shape=(jax.ShapeDtypeStruct((slots, size, size), jnp.float32), flat, flat),
        in_specs=[smem] + [vmem] * (PIECES + 2),
        out_specs=(pl.BlockSpec(memory_space=pltpu.HBM), vmem, vmem),
        scratch_shapes=[pltpu.VMEM((slots, size, size), jnp.float32), pltpu.SemaphoreType.DMA((slots,))],
        compiler_params=pltpu.CompilerParams(vmem_limit_bytes=16 * MIB),
        name="scaled",
    )(meta, *stay(held), row_last, col_last)
    return row_out.reshape(-1), col_out.reshape(-1), scaled[None, None]


def solution(mesh):
    zs, cs, ds = (mesh.shape[a] for a in AXES)
    xs = 4
    sizes = (zs, xs, cs // xs)
    in_specs = (
        P("row", "col", "depth", None, None),
        P("row", "col", "depth"),
        P("row", "col", "depth"),
        P("row", "col", "depth"),
    )
    out_specs = (P("row"), P("col"), P("row", "col", "depth", None, None))
    return jax.shard_map(
        functools.partial(shards, sizes), mesh=mesh, in_specs=in_specs, out_specs=out_specs, check_vma=False
    )
```

```python
import functools
import math

import jax
import jax.numpy as jnp
from jax import lax
from jax.experimental import pallas as pl
from jax.experimental.pallas import tpu as pltpu
from jax.sharding import PartitionSpec as P

BLOCKS = 128
EPS = 1e-06
AXES = ("row", "col", "depth")
LOAD_GROUP = 4
SWEEP_GROUP = 16
CHIP_GROUP = 8
COPY_GROUP = 4
PIECES = 3
ORDER = (1, 3, 2)
MIB = 1024 * 1024


def scale_row(meta_ref, slots, t):
    return meta_ref[t], meta_ref[slots + t]


def fold(summed):
    return (lambda a, b: a + b) if summed else jnp.maximum


def tile_partials(values, row_vec, col_vec, want_row, want_col, summed):
    join = fold(summed)
    reduce = jnp.sum if summed else jnp.max
    row_halves = []
    col_acc = None
    for h in range(2):
        rows = slice(h * 128, (h + 1) * 128)
        left = jnp.abs(values[rows, 0:128])
        right = jnp.abs(values[rows, 128:256])
        if want_row:
            if col_vec is None:
                part = join(left, right)
            else:
                part = join(left * col_vec[:, 0:128], right * col_vec[:, 128:256])
            row_halves.append(reduce(part.T, axis=0, keepdims=True))
        if want_col:
            if row_vec is not None:
                factor = jnp.broadcast_to(row_vec[:, rows], (128, 128)).T
                left = left * factor
                right = right * factor
            both = [reduce(x.reshape(16, 8, 128), axis=0) for x in (left, right)]
            col_acc = both if col_acc is None else [join(a, b) for a, b in zip(col_acc, both)]
    row_out = jnp.concatenate(row_halves, axis=1) if want_row else None
    col_out = None
    if want_col:
        col_out = jnp.concatenate([reduce(a, axis=0, keepdims=True) for a in col_acc], axis=1)
    return row_out, col_out


def clear(*accs):
    for acc in accs:
        if acc is not None:
            acc[...] = jnp.zeros_like(acc)


def sweep(slots, group, meta_ref, tiles_ref, offset, row_ref, col_ref, row_acc, col_acc, summed, before=None, step=1):
    want_row, want_col = row_acc is not None, col_acc is not None
    join = fold(summed)
    held = tiles_ref.shape[0]
    group = math.gcd(held, group)
    count = jnp.clip(meta_ref[2 * slots] - offset, 0, held)

    def body(g, carry):
        found = []
        if before is not None:
            for k in range(0, group, step):
                before(g * group + k)
        for k in range(group):
            t = g * group + k
            row, col = meta_ref[offset + t], meta_ref[slots + offset + t]
            row_vec = None if row_ref is None else row_ref[pl.ds(row, 1), :]
            col_vec = None if col_ref is None else col_ref[pl.ds(col, 1), :]
            values = tiles_ref.at[t]
            row_out, col_out = tile_partials(values, row_vec, col_vec, want_row, want_col, summed)
            live = t < count
            if want_row:
                row_out = jnp.where(live, row_out, 0.0)
            if want_col:
                col_out = jnp.where(live, col_out, 0.0)
            found.append((row, col, row_out, col_out))
        for row, col, row_out, col_out in found:
            if want_row:
                row_acc[pl.ds(row, 1), :] = join(row_acc[pl.ds(row, 1), :], row_out)
            if want_col:
                col_acc[pl.ds(col, 1), :] = join(col_acc[pl.ds(col, 1), :], col_out)
        return carry

    lax.fori_loop(0, (count + group - 1) // group, body, 0)


def split(core, row_acc, col_acc, mine_ref, other_ref):
    first = core == 0
    mine_ref[...] = jnp.where(first, row_acc[...], col_acc[...])
    other_ref[...] = jnp.where(first, col_acc[...], row_acc[...])


def load_kernel(slots, size, meta_ref, hbm_ref, *refs):
    held, (mine_ref, other_ref, first_ref, row_acc, col_acc, sem) = refs[:PIECES], refs[PIECES:]
    count = meta_ref[2 * slots]
    step = math.gcd(size, COPY_GROUP)
    group = math.gcd(size, LOAD_GROUP)

    def copy(ref, offset, g):
        return pltpu.make_async_copy(
            hbm_ref.at[pl.ds(offset + g * step, step)], ref.at[pl.ds(g * step, step)], sem.at[offset // step + g]
        )

    for place, ref in enumerate(held):

        def start(g, carry, ref=ref, offset=place * size):
            copy(ref, offset, g).start()
            return carry

        lax.fori_loop(0, (jnp.clip(count - place * size, 0, size) + step - 1) // step, start, 0)
    first_ref[...] = jnp.where(meta_ref[2 * slots + 1] == 0, jnp.ones_like(first_ref), 0.0)
    clear(row_acc, col_acc)
    for place, ref in enumerate(held):

        def before(t, ref=ref, offset=place * size):
            @pl.when(offset + t < count)
            def _():
                copy(ref, offset, t // step).wait()

        sweep(slots, group, meta_ref, ref, place * size, None, None, row_acc, col_acc, False, before, step)
    split(meta_ref[2 * slots + 1], row_acc, col_acc, mine_ref, other_ref)


def row_kernel(slots, size, meta_ref, *refs):
    held, (s_ref, g_ref, part_ref, col_ref) = refs[:PIECES], refs[PIECES:]
    first = meta_ref[2 * slots + 1] == 0
    col_ref[...] = jnp.where(first, g_ref[...], s_ref[...])
    clear(part_ref)
    for place, ref in enumerate(held):
        sweep(slots, SWEEP_GROUP, meta_ref, ref, place * size, None, col_ref, part_ref, None, False)


def col_kernel(slots, size, meta_ref, *refs):
    held, (s_ref, g_ref, part_ref, row_ref) = refs[:PIECES], refs[PIECES:]
    first = meta_ref[2 * slots + 1] == 0
    row_ref[...] = jnp.where(first, s_ref[...], g_ref[...])
    clear(part_ref)
    for place, ref in enumerate(held):
        sweep(slots, SWEEP_GROUP, meta_ref, ref, place * size, row_ref, None, None, part_ref, False)


def chip_kernel(slots, size, kinds, summed, meta_ref, twin_ref, *refs):
    held, twins, (s_ref, part_ref) = refs[:PIECES], refs[PIECES : 2 * PIECES], refs[2 * PIECES :]
    core = meta_ref[2 * slots + 1]
    for place, kind in enumerate(kinds):

        @pl.when(core == place)
        def _():
            if kind is None:
                part_ref[...] = s_ref[...]
                return
            clear(part_ref)
            for meta, pieces in ((meta_ref, held), (twin_ref, twins)):
                for spot, ref in enumerate(pieces):
                    if kind == "rows":
                        sweep(slots, CHIP_GROUP, meta, ref, spot * size, None, s_ref, part_ref, None, summed)
                    else:
                        sweep(slots, CHIP_GROUP, meta, ref, spot * size, s_ref, None, None, part_ref, summed)


def final_kernel(slots, size, meta_ref, *refs):
    held, (row_ref, col_ref, out_ref, row_out, col_out, done, sem) = refs[:PIECES], refs[PIECES:]
    count = meta_ref[2 * slots]
    group = math.gcd(size, COPY_GROUP)

    def copy(g):
        span = pl.ds(g * group, group)
        return pltpu.make_async_copy(done.at[span], out_ref.at[span], sem.at[g])

    for place, ref in enumerate(held):
        offset = place * size

        def fill(g, carry, ref=ref, offset=offset):
            for k in range(group):
                t = g * group + k
                slot = offset + t
                live = slot < count
                row_vec = row_ref[pl.ds(meta_ref[slot], 1), :]
                col_vec = col_ref[pl.ds(meta_ref[slots + slot], 1), :]
                for h in range(2):
                    rows = slice(h * 128, (h + 1) * 128)
                    factor = jnp.broadcast_to(row_vec[:, rows], (128, 128)).T
                    for w in range(2):
                        cols = slice(w * 128, (w + 1) * 128)
                        scaled = ref[t, rows, cols] * factor * col_vec[:, cols]
                        done[slot, rows, cols] = jnp.where(live, scaled, 0.0)
            copy(offset // group + g).start()
            return carry

        full = (jnp.clip(count - offset, 0, size) + group - 1) // group
        lax.fori_loop(0, full, fill, 0)

        def zero(g, carry, offset=offset):
            done[pl.ds(offset + g * group, group)] = jnp.zeros((group,) + done.shape[1:], jnp.float32)
            copy(offset // group + g).start()
            return carry

        lax.fori_loop(full, size // group, zero, 0)
    for vec_ref, flat in ((row_ref, row_out), (col_ref, col_out)):
        for w in range(2):
            flat[pl.ds(w, BLOCKS, 2), :] = vec_ref[:, w * 128 : (w + 1) * 128]

    def finish(g, carry):
        copy(g).wait()
        return carry

    lax.fori_loop(0, slots // group, finish, 0)


def shards(sizes, tiles, tile_rows, tile_cols, tile_count):
    zs, xs, ys = sizes
    values = tiles[0, 0]
    slots, size = values.shape[0], values.shape[1]
    core = lax.axis_index("depth")
    meta = jnp.concatenate(
        [tile_rows[0, 0], tile_cols[0, 0], tile_count[0, 0], core[None].astype(jnp.int32)]
    )

    smem = pl.BlockSpec(memory_space=pltpu.SMEM)
    vmem = pl.BlockSpec(memory_space=pltpu.VMEM)
    params = pltpu.CompilerParams(vmem_limit_bytes=8 * MIB)
    vec = jax.ShapeDtypeStruct((BLOCKS, size), jnp.float32)
    acc = pltpu.VMEM((BLOCKS, size), jnp.float32)
    part_slots = slots // PIECES
    kept = pltpu.VMEM((part_slots, size, size), jnp.float32)

    def spots(move):
        pairs = []
        for z in range(zs):
            for x in range(xs):
                for y in range(ys):
                    for d in range(2):
                        pairs.append((index(z, x, y, d), index(*move(z, x, y, d))))
        return pairs

    def index(z, x, y, d):
        return ((z * xs + x) * ys + y) * 2 + d

    steps = {
        "x": lambda z, x, y, d, s: (z, x ^ s, y, d),
        "y": lambda z, x, y, d, s: (z, x, y ^ s, d),
        "z": lambda z, x, y, d, s: (z ^ s, x, y, d),
    }

    def slot(v, first_axis, second_axis):
        parts = [v]
        for s in ORDER:
            def move(z, x, y, d, s=s):
                return steps[first_axis if d == 0 else second_axis](z, x, y, d, s)
            parts.append(lax.ppermute(v, AXES, spots(move)))
        return parts

    def top(parts):
        return jnp.maximum(jnp.maximum(parts[0], parts[1]), jnp.maximum(parts[2], parts[3]))

    def total(parts):
        return (parts[0] + parts[1]) + (parts[2] + parts[3])

    def next_factor(old, partial):
        return old * lax.rsqrt(old * partial + EPS)

    swap = lambda v: lax.ppermute(v, "depth", [(0, 1), (1, 0)])

    def pick(a, b):
        return jnp.where(is_first > 0.5, a, b)

    *held, mine, other, is_first = pl.pallas_call(
        functools.partial(load_kernel, slots, part_slots),
        out_shape=(kept,) * PIECES + (vec, vec, vec),
        in_specs=[smem, pl.BlockSpec(memory_space=pltpu.HBM)],
        out_specs=(vmem,) * (PIECES + 3),
        scratch_shapes=[acc, acc, pltpu.SemaphoreType.DMA((slots,))],
        compiler_params=params,
        name="load",
    )(meta, pltpu.with_memory_space_constraint(values, pltpu.HBM))

    def stay(pieces):
        return [pltpu.with_memory_space_constraint(v, pltpu.VMEM) for v in pieces]

    twins = []

    def share(after):
        v, after = lax.optimization_barrier((held[len(twins)], after))
        twins.append(swap(v))
        return after

    def shared(before):
        twins[-1], before = lax.optimization_barrier((twins[-1], before))
        return before

    def own(kernel, name):
        def run(*args):
            return pl.pallas_call(
                functools.partial(kernel, slots, part_slots),
                out_shape=(vec, vec),
                in_specs=[smem] + [vmem] * (PIECES + 2),
                out_specs=(vmem, vmem),
                compiler_params=params,
                name=name,
            )(meta, *stay(held), *args)
        return run

    def chip(kinds, summed, name, s):
        return pl.pallas_call(
            functools.partial(chip_kernel, slots, part_slots, kinds, summed),
            out_shape=vec,
            in_specs=[smem, smem] + [vmem] * (2 * PIECES + 1),
            out_specs=vmem,
            compiler_params=params,
            name=name,
        )(meta, twin, *stay(held), *stay(twins), s)

    def late_swap(v, parts):
        return swap(lax.optimization_barrier((v, parts[2]))[0])

    twin = swap(meta)
    m = jnp.maximum(mine, swap(other))
    m = share(m)
    u = top(slot(m, "x", "z"))
    s = pick(u, lax.rsqrt(u + EPS))
    s = shared(s)
    part, col_1 = own(row_kernel, "rows")(s, swap(s))
    m = pick(s, jnp.maximum(part, swap(part)))
    m = share(m)
    u = top(slot(m, "y", "x"))
    s = pick(lax.rsqrt(u + EPS), u)
    s = shared(s)
    part, row_1 = own(col_kernel, "cols")(s, swap(s))
    m = share(pick(jnp.maximum(part, swap(part)), s))
    u = top(slot(m, "z", "y"))
    now_2 = next_factor(pick(col_1, row_1), u)

    parts = slot(chip(("rows", "cols"), False, "chip_both", now_2), "x", "z")
    old_2 = late_swap(now_2, parts)
    u = top(parts)
    s = pick(u, next_factor(old_2, u))
    col_3 = swap(s)
    u = top(slot(chip((None, "rows"), False, "chip_rows", s), "y", "x"))
    s = pick(next_factor(old_2, u), u)
    row_3 = swap(s)
    u = top(slot(chip(("cols", None), False, "chip_cols", s), "z", "y"))
    now_4 = next_factor(pick(col_3, row_3), u)
    parts = slot(chip(("rows", "cols"), True, "chip_sums", now_4), "x", "z")
    old_4 = late_swap(now_4, parts)
    u = total(parts)
    s = pick(u, next_factor(old_4, u))
    col_last = pick(swap(s), s)
    u = total(slot(s, "y", "x"))
    s = next_factor(old_4, u)
    row_last = pick(s, swap(s))

    flat = jax.ShapeDtypeStruct((2 * BLOCKS, size // 2), jnp.float32)
    scaled, row_out, col_out = pl.pallas_call(
        functools.partial(final_kernel, slots, part_slots),
        out_shape=(jax.ShapeDtypeStruct((slots, size, size), jnp.float32), flat, flat),
        in_specs=[smem] + [vmem] * (PIECES + 2),
        out_specs=(pl.BlockSpec(memory_space=pltpu.HBM), vmem, vmem),
        scratch_shapes=[pltpu.VMEM((slots, size, size), jnp.float32), pltpu.SemaphoreType.DMA((slots,))],
        compiler_params=pltpu.CompilerParams(vmem_limit_bytes=16 * MIB),
        name="scaled",
    )(meta, *stay(held), row_last, col_last)
    return row_out.reshape(-1), col_out.reshape(-1), scaled[None, None]


def solution(mesh):
    zs, cs, ds = (mesh.shape[a] for a in AXES)
    xs = 4
    sizes = (zs, xs, cs // xs)
    in_specs = (
        P("row", "col", "depth", None, None),
        P("row", "col", "depth"),
        P("row", "col", "depth"),
        P("row", "col", "depth"),
    )
    out_specs = (P("row"), P("col"), P("row", "col", "depth", None, None))
    return jax.shard_map(
        functools.partial(shards, sizes), mesh=mesh, in_specs=in_specs, out_specs=out_specs, check_vma=False
    )
```

```python
import functools
import math

import jax
import jax.numpy as jnp
from jax import lax
from jax.experimental import pallas as pl
from jax.experimental.pallas import tpu as pltpu
from jax.sharding import PartitionSpec as P

BLOCKS = 128
EPS = 1e-06
AXES = ("row", "col", "depth")
LOAD_GROUP = 4
SWEEP_GROUP = 8
CHIP_GROUP = 8
COPY_GROUP = 4
PIECES = 3
ORDER = (1, 3, 2)
MIB = 1024 * 1024


def scale_row(meta_ref, slots, t):
    return meta_ref[t], meta_ref[slots + t]


def fold(summed):
    return (lambda a, b: a + b) if summed else jnp.maximum


def tile_partials(values, row_vec, col_vec, want_row, want_col, summed):
    join = fold(summed)
    reduce = jnp.sum if summed else jnp.max
    row_halves = []
    col_acc = None
    for h in range(2):
        rows = slice(h * 128, (h + 1) * 128)
        left = jnp.abs(values[rows, 0:128])
        right = jnp.abs(values[rows, 128:256])
        if want_row:
            if col_vec is None:
                part = join(left, right)
            else:
                part = join(left * col_vec[:, 0:128], right * col_vec[:, 128:256])
            row_halves.append(reduce(part.T, axis=0, keepdims=True))
        if want_col:
            if row_vec is not None:
                factor = jnp.broadcast_to(row_vec[:, rows], (128, 128)).T
                left = left * factor
                right = right * factor
            both = [reduce(x.reshape(16, 8, 128), axis=0) for x in (left, right)]
            col_acc = both if col_acc is None else [join(a, b) for a, b in zip(col_acc, both)]
    row_out = jnp.concatenate(row_halves, axis=1) if want_row else None
    col_out = None
    if want_col:
        col_out = jnp.concatenate([reduce(a, axis=0, keepdims=True) for a in col_acc], axis=1)
    return row_out, col_out


def clear(*accs):
    for acc in accs:
        if acc is not None:
            acc[...] = jnp.zeros_like(acc)


def sweep(slots, group, meta_ref, tiles_ref, offset, row_ref, col_ref, row_acc, col_acc, summed, before=None, step=1):
    want_row, want_col = row_acc is not None, col_acc is not None
    join = fold(summed)
    held = tiles_ref.shape[0]
    group = math.gcd(held, group)
    count = jnp.clip(meta_ref[2 * slots] - offset, 0, held)

    def body(g, carry):
        found = []
        if before is not None:
            for k in range(0, group, step):
                before(g * group + k)
        for k in range(group):
            t = g * group + k
            row, col = meta_ref[offset + t], meta_ref[slots + offset + t]
            row_vec = None if row_ref is None else row_ref[pl.ds(row, 1), :]
            col_vec = None if col_ref is None else col_ref[pl.ds(col, 1), :]
            values = tiles_ref.at[t]
            row_out, col_out = tile_partials(values, row_vec, col_vec, want_row, want_col, summed)
            live = t < count
            if want_row:
                row_out = jnp.where(live, row_out, 0.0)
            if want_col:
                col_out = jnp.where(live, col_out, 0.0)
            found.append((row, col, row_out, col_out))
        for row, col, row_out, col_out in found:
            if want_row:
                row_acc[pl.ds(row, 1), :] = join(row_acc[pl.ds(row, 1), :], row_out)
            if want_col:
                col_acc[pl.ds(col, 1), :] = join(col_acc[pl.ds(col, 1), :], col_out)
        return carry

    lax.fori_loop(0, (count + group - 1) // group, body, 0)


def split(core, row_acc, col_acc, mine_ref, other_ref):
    first = core == 0
    mine_ref[...] = jnp.where(first, row_acc[...], col_acc[...])
    other_ref[...] = jnp.where(first, col_acc[...], row_acc[...])


def load_kernel(slots, size, meta_ref, hbm_ref, *refs):
    held, (mine_ref, other_ref, first_ref, row_acc, col_acc, sem) = refs[:PIECES], refs[PIECES:]
    count = meta_ref[2 * slots]
    step = math.gcd(size, COPY_GROUP)
    group = math.gcd(size, LOAD_GROUP)

    def copy(ref, offset, g):
        return pltpu.make_async_copy(
            hbm_ref.at[pl.ds(offset + g * step, step)], ref.at[pl.ds(g * step, step)], sem.at[offset // step + g]
        )

    for place, ref in enumerate(held):

        def start(g, carry, ref=ref, offset=place * size):
            copy(ref, offset, g).start()
            return carry

        lax.fori_loop(0, (jnp.clip(count - place * size, 0, size) + step - 1) // step, start, 0)
    first_ref[...] = jnp.where(meta_ref[2 * slots + 1] == 0, jnp.ones_like(first_ref), 0.0)
    clear(row_acc, col_acc)
    for place, ref in enumerate(held):

        def before(t, ref=ref, offset=place * size):
            @pl.when(offset + t < count)
            def _():
                copy(ref, offset, t // step).wait()

        sweep(slots, group, meta_ref, ref, place * size, None, None, row_acc, col_acc, False, before, step)
    split(meta_ref[2 * slots + 1], row_acc, col_acc, mine_ref, other_ref)


def row_kernel(slots, size, meta_ref, *refs):
    held, (s_ref, g_ref, part_ref, col_ref) = refs[:PIECES], refs[PIECES:]
    first = meta_ref[2 * slots + 1] == 0
    col_ref[...] = jnp.where(first, g_ref[...], s_ref[...])
    clear(part_ref)
    for place, ref in enumerate(held):
        sweep(slots, SWEEP_GROUP, meta_ref, ref, place * size, None, col_ref, part_ref, None, False)


def col_kernel(slots, size, meta_ref, *refs):
    held, (s_ref, g_ref, part_ref, row_ref) = refs[:PIECES], refs[PIECES:]
    first = meta_ref[2 * slots + 1] == 0
    row_ref[...] = jnp.where(first, s_ref[...], g_ref[...])
    clear(part_ref)
    for place, ref in enumerate(held):
        sweep(slots, SWEEP_GROUP, meta_ref, ref, place * size, row_ref, None, None, part_ref, False)


def chip_kernel(slots, size, kinds, summed, meta_ref, twin_ref, *refs):
    held, twins, (s_ref, part_ref) = refs[:PIECES], refs[PIECES : 2 * PIECES], refs[2 * PIECES :]
    core = meta_ref[2 * slots + 1]
    for place, kind in enumerate(kinds):

        @pl.when(core == place)
        def _():
            if kind is None:
                part_ref[...] = s_ref[...]
                return
            clear(part_ref)
            for meta, pieces in ((meta_ref, held), (twin_ref, twins)):
                for spot, ref in enumerate(pieces):
                    if kind == "rows":
                        sweep(slots, CHIP_GROUP, meta, ref, spot * size, None, s_ref, part_ref, None, summed)
                    else:
                        sweep(slots, CHIP_GROUP, meta, ref, spot * size, s_ref, None, None, part_ref, summed)


def final_kernel(slots, size, meta_ref, *refs):
    held, (row_ref, col_ref, out_ref, row_out, col_out, done, sem) = refs[:PIECES], refs[PIECES:]
    count = meta_ref[2 * slots]
    group = math.gcd(size, COPY_GROUP)

    def copy(g):
        span = pl.ds(g * group, group)
        return pltpu.make_async_copy(done.at[span], out_ref.at[span], sem.at[g])

    for place, ref in enumerate(held):
        offset = place * size

        def fill(g, carry, ref=ref, offset=offset):
            for k in range(group):
                t = g * group + k
                slot = offset + t
                live = slot < count
                row_vec = row_ref[pl.ds(meta_ref[slot], 1), :]
                col_vec = col_ref[pl.ds(meta_ref[slots + slot], 1), :]
                for h in range(2):
                    rows = slice(h * 128, (h + 1) * 128)
                    factor = jnp.broadcast_to(row_vec[:, rows], (128, 128)).T
                    for w in range(2):
                        cols = slice(w * 128, (w + 1) * 128)
                        scaled = ref[t, rows, cols] * factor * col_vec[:, cols]
                        done[slot, rows, cols] = jnp.where(live, scaled, 0.0)
            copy(offset // group + g).start()
            return carry

        full = (jnp.clip(count - offset, 0, size) + group - 1) // group
        lax.fori_loop(0, full, fill, 0)

        def zero(g, carry, offset=offset):
            done[pl.ds(offset + g * group, group)] = jnp.zeros((group,) + done.shape[1:], jnp.float32)
            copy(offset // group + g).start()
            return carry

        lax.fori_loop(full, size // group, zero, 0)
    for vec_ref, flat in ((row_ref, row_out), (col_ref, col_out)):
        for w in range(2):
            flat[pl.ds(w, BLOCKS, 2), :] = vec_ref[:, w * 128 : (w + 1) * 128]

    def finish(g, carry):
        copy(g).wait()
        return carry

    lax.fori_loop(0, slots // group, finish, 0)


def shards(sizes, tiles, tile_rows, tile_cols, tile_count):
    zs, xs, ys = sizes
    values = tiles[0, 0]
    slots, size = values.shape[0], values.shape[1]
    core = lax.axis_index("depth")
    meta = jnp.concatenate(
        [tile_rows[0, 0], tile_cols[0, 0], tile_count[0, 0], core[None].astype(jnp.int32)]
    )

    smem = pl.BlockSpec(memory_space=pltpu.SMEM)
    vmem = pl.BlockSpec(memory_space=pltpu.VMEM)
    params = pltpu.CompilerParams(vmem_limit_bytes=8 * MIB)
    vec = jax.ShapeDtypeStruct((BLOCKS, size), jnp.float32)
    acc = pltpu.VMEM((BLOCKS, size), jnp.float32)
    part_slots = slots // PIECES
    kept = pltpu.VMEM((part_slots, size, size), jnp.float32)

    def spots(move):
        pairs = []
        for z in range(zs):
            for x in range(xs):
                for y in range(ys):
                    for d in range(2):
                        pairs.append((index(z, x, y, d), index(*move(z, x, y, d))))
        return pairs

    def index(z, x, y, d):
        return ((z * xs + x) * ys + y) * 2 + d

    steps = {
        "x": lambda z, x, y, d, s: (z, x ^ s, y, d),
        "y": lambda z, x, y, d, s: (z, x, y ^ s, d),
        "z": lambda z, x, y, d, s: (z ^ s, x, y, d),
    }

    def slot(v, first_axis, second_axis):
        parts = [v]
        for s in ORDER:
            def move(z, x, y, d, s=s):
                return steps[first_axis if d == 0 else second_axis](z, x, y, d, s)
            parts.append(lax.ppermute(v, AXES, spots(move)))
        return parts

    def top(parts):
        return jnp.maximum(jnp.maximum(parts[0], parts[1]), jnp.maximum(parts[2], parts[3]))

    def total(parts):
        return (parts[0] + parts[1]) + (parts[2] + parts[3])

    def next_factor(old, partial):
        return old * lax.rsqrt(old * partial + EPS)

    swap = lambda v: lax.ppermute(v, "depth", [(0, 1), (1, 0)])

    def pick(a, b):
        return jnp.where(is_first > 0.5, a, b)

    *held, mine, other, is_first = pl.pallas_call(
        functools.partial(load_kernel, slots, part_slots),
        out_shape=(kept,) * PIECES + (vec, vec, vec),
        in_specs=[smem, pl.BlockSpec(memory_space=pltpu.HBM)],
        out_specs=(vmem,) * (PIECES + 3),
        scratch_shapes=[acc, acc, pltpu.SemaphoreType.DMA((slots,))],
        compiler_params=params,
        name="load",
    )(meta, pltpu.with_memory_space_constraint(values, pltpu.HBM))

    def stay(pieces):
        return [pltpu.with_memory_space_constraint(v, pltpu.VMEM) for v in pieces]

    twins = []

    def share(after):
        v, after = lax.optimization_barrier((held[len(twins)], after))
        twins.append(swap(v))
        return after

    def shared(before):
        twins[-1], before = lax.optimization_barrier((twins[-1], before))
        return before

    def own(kernel, name):
        def run(*args):
            return pl.pallas_call(
                functools.partial(kernel, slots, part_slots),
                out_shape=(vec, vec),
                in_specs=[smem] + [vmem] * (PIECES + 2),
                out_specs=(vmem, vmem),
                compiler_params=params,
                name=name,
            )(meta, *stay(held), *args)
        return run

    def chip(kinds, summed, name, s):
        return pl.pallas_call(
            functools.partial(chip_kernel, slots, part_slots, kinds, summed),
            out_shape=vec,
            in_specs=[smem, smem] + [vmem] * (2 * PIECES + 1),
            out_specs=vmem,
            compiler_params=params,
            name=name,
        )(meta, twin, *stay(held), *stay(twins), s)

    def late_swap(v, parts):
        return swap(lax.optimization_barrier((v, parts[2]))[0])

    twin = swap(meta)
    m = jnp.maximum(mine, swap(other))
    m = share(m)
    u = top(slot(m, "x", "z"))
    s = pick(u, lax.rsqrt(u + EPS))
    s = shared(s)
    part, col_1 = own(row_kernel, "rows")(s, swap(s))
    m = pick(s, jnp.maximum(part, swap(part)))
    m = share(m)
    u = top(slot(m, "y", "x"))
    s = pick(lax.rsqrt(u + EPS), u)
    s = shared(s)
    part, row_1 = own(col_kernel, "cols")(s, swap(s))
    m = share(pick(jnp.maximum(part, swap(part)), s))
    u = top(slot(m, "z", "y"))
    now_2 = next_factor(pick(col_1, row_1), u)

    parts = slot(chip(("rows", "cols"), False, "chip_both", now_2), "x", "z")
    old_2 = late_swap(now_2, parts)
    u = top(parts)
    s = pick(u, next_factor(old_2, u))
    col_3 = swap(s)
    u = top(slot(chip((None, "rows"), False, "chip_rows", s), "y", "x"))
    s = pick(next_factor(old_2, u), u)
    row_3 = swap(s)
    u = top(slot(chip(("cols", None), False, "chip_cols", s), "z", "y"))
    now_4 = next_factor(pick(col_3, row_3), u)
    parts = slot(chip(("rows", "cols"), True, "chip_sums", now_4), "x", "z")
    old_4 = late_swap(now_4, parts)
    u = total(parts)
    s = pick(u, next_factor(old_4, u))
    col_last = pick(swap(s), s)
    u = total(slot(s, "y", "x"))
    s = next_factor(old_4, u)
    row_last = pick(s, swap(s))

    flat = jax.ShapeDtypeStruct((2 * BLOCKS, size // 2), jnp.float32)
    scaled, row_out, col_out = pl.pallas_call(
        functools.partial(final_kernel, slots, part_slots),
        out_shape=(jax.ShapeDtypeStruct((slots, size, size), jnp.float32), flat, flat),
        in_specs=[smem] + [vmem] * (PIECES + 2),
        out_specs=(pl.BlockSpec(memory_space=pltpu.HBM), vmem, vmem),
        scratch_shapes=[pltpu.VMEM((slots, size, size), jnp.float32), pltpu.SemaphoreType.DMA((slots,))],
        compiler_params=pltpu.CompilerParams(vmem_limit_bytes=16 * MIB),
        name="scaled",
    )(meta, *stay(held), row_last, col_last)
    return row_out.reshape(-1), col_out.reshape(-1), scaled[None, None]


def solution(mesh):
    zs, cs, ds = (mesh.shape[a] for a in AXES)
    xs = 4
    sizes = (zs, xs, cs // xs)
    in_specs = (
        P("row", "col", "depth", None, None),
        P("row", "col", "depth"),
        P("row", "col", "depth"),
        P("row", "col", "depth"),
    )
    out_specs = (P("row"), P("col"), P("row", "col", "depth", None, None))
    return jax.shard_map(
        functools.partial(shards, sizes), mesh=mesh, in_specs=in_specs, out_specs=out_specs, check_vma=False
    )
```
